512 devices in a mesh: expert: 64 (over z_hi, x, y), dp: 8 (over z_lo, core).
Axes of the slice: x: 4, y: 4, z: 16 (z_hi: 4, z_lo: 4; z = z_hi * 4 + z_lo), core: 2. Of those that a mesh axis runs over, the one named last changes fastest.
Arguments:
- hidden: bfloat16 [65536, 1, 1024], P(('expert', 'dp')), may hold values from -6 to 6
- probs: float32 [65536, 1], P(('expert', 'dp')), may hold values from 0.05 to 1
- expert_ids: int32 [65536, 1], P(('expert', 'dp')), may hold values from 0 to 63; in each aligned block of 128 rows (0 to 127, 128 to 255, ...) at most 4 rows name the same one
- swap_plan: int32 [64], replicated, may hold values from 0 to 1, as said below
- down_weight: bfloat16 [64, 1024, 4096], P('expert', None, 'dp'), may hold values from -0.1875 to 0.1875
- out_grad: bfloat16 [65536, 4096], P(('expert', 'dp')), may hold values from -0.29882812 to 0.29882812
Outputs:
- mixed: bfloat16 [65536, 4096], P(('expert', 'dp'))
- hidden_grad: bfloat16 [65536, 1, 1024], P(('expert', 'dp'))
- prob_grad: float32 [65536, 1], P(('expert', 'dp'))
- weight_grad: bfloat16 [64, 1024, 4096], P('expert', None, 'dp')
The draws below stay inside these ranges and needn't reach their ends.
Inputs may be any that keep to these rules, and one draw needn't show every extreme that they name: `expert_ids`: each device's 128 tokens name one expert at most 4 times. swap_plan[e] equals swap_plan[e + 32] for e below 32.
All inputs are finite; a program needn't handle non-finite values.
Results may differ from the reference program's by a relative error of at most 0.017.
Values may be sent and summed in bfloat16 or wider, within the bound.
A program may use at most 64 MiB of HBM per device.

```python
import math
import jax
import jax.numpy as jnp
import numpy as np
from jax import lax

D = 4096
FF = 1024
TOP = 1
TOK_DEV = 128
EXPERTS = 64
CAP = 4
TOKENS = 65536
N_DP = 8


def draw_swap_plan(key, part):
    half = EXPERTS // 2
    paired = jax.random.randint(key, (half,), 0, 2, dtype=jnp.int32)
    paired = paired.at[0].set(1).at[1].set(0)
    return jnp.concatenate([paired, paired])


def block_levels(stream_key, dims, pieces, low, top_value):
    loudness = 1.0
    for axis_at, blocks in pieces:
        steps = jax.random.uniform(jax.random.fold_in(jax.random.fold_in(stream_key, 6), axis_at), (blocks,), jnp.float32, low / len(pieces), top_value / len(pieces))
        loudness = loudness * jnp.repeat(jnp.exp(steps), dims[axis_at] // blocks).reshape((-1,) + (1,) * (len(dims) - 1 - axis_at))
    return loudness


def deal_out(own_key, own, number, rows, count, top, bound, skew):
    ranking = jax.random.permutation(own_key, count)
    heavy_load, ordinary = shares(count, rows * top, bound, skew, True), shares(count, rows * top, bound, skew, False)
    places = jnp.arange(count)

    def named(lengths, rotation):
        used = int((lengths > 0).sum())
        fixed = max(1, used // 4)
        shifted = fixed + (places - fixed + rotation * (used - fixed)) % max(1, count - fixed)
        return jnp.zeros((count,), jnp.int32).at[ranking[jnp.where(places < fixed, places, shifted)]].set(jnp.asarray(lengths, jnp.int32))

    lengths = jnp.where(number % 4 == 0, named(heavy_load, number // 4), named(ordinary, number - number // 4 - 1))
    mixed = jax.random.permutation(jax.random.fold_in(own, 3), count)
    source_of, sink = mixed[0:count // 2 * 2:2], mixed[1:count // 2 * 2:2]
    slack = jnp.minimum(lengths[source_of] - 1, bound - lengths[sink]) // 2
    slack = jnp.where((source_of == ranking[0]) | (sink == ranking[0]) | (lengths[sink] == 0), 0, jnp.maximum(slack, 0))
    shifted = jax.random.randint(jax.random.fold_in(own, 4), (count // 2,), 0, 1 << 20) % (slack + 1)
    lengths = lengths.at[source_of].add(-shifted).at[sink].add(shifted)
    members = jnp.searchsorted(jnp.cumsum(lengths), jnp.arange(rows * top), side="right").astype(jnp.int32)
    grid = members.reshape(top, rows).T
    grid = grid[jax.random.permutation(jax.random.fold_in(own, 1), rows)]
    rotation = jax.random.randint(jax.random.fold_in(own, 2), (rows, 1), 0, top)
    return jnp.take_along_axis(grid, (jnp.arange(top)[None, :] + rotation) % top, axis=1)


def shares(number_of, total, most, skew, full):
    weights = [(1 << 20) // math.isqrt(standing ** skew) + 1 for standing in range(1, number_of + 1)]
    largest = most if full else min(most, max(-(-total // number_of), total * weights[0] // sum(weights)))
    least = 1 if total - largest >= number_of - 1 else 0
    counts, rest = [largest] + [least] * (number_of - 1), total - largest - least * (number_of - 1)
    while rest > 0:
        free = [i for i in range(1, number_of) if counts[i] < largest] or [i for i in range(1, number_of) if counts[i] < most]
        pool, remaining = sum([weights[i] for i in free]), rest
        for i in free:
            addition = min(most - counts[i], max(1, remaining * weights[i] // pool), rest)
            counts[i] = counts[i] + addition
            rest = rest - addition
    return np.array(counts)


def scatter_about(own_key, shape, deviation, most, shards=(), held_as=jnp.bfloat16):
    drawn = deviation * jax.random.normal(own_key, shape, jnp.float32)
    if shards:
        drawn = drawn * block_levels(own_key, shape, shards, -0.22, 0.18)
    return jnp.clip(drawn, -most, most).astype(held_as)


def setup_inputs(seed: int = 0) -> dict:
    splits = jax.random.split(jax.random.key(seed), 7)
    hidden = scatter_about(splits[0], (TOKENS, TOP, FF), 1.0, 6.0, ((0, 512),))
    probs = jnp.clip(0.05 + 0.95 * jax.random.uniform(splits[1], (TOKENS, TOP), jnp.float32) ** block_levels(splits[1], (TOKENS, TOP), ((0, 512),), -0.2, 0.2), 0.05, 1.0)
    expert_ids_keys = jax.random.split(jax.random.fold_in(splits[2], 1), TOKENS // TOK_DEV)
    expert_ids_turns = jax.random.permutation(jax.random.fold_in(splits[2], 3), TOKENS // TOK_DEV)
    expert_ids = jax.vmap(lambda own, number: deal_out(jax.random.fold_in(splits[2], 2), own, number, TOK_DEV, EXPERTS, TOP, CAP, 2))(expert_ids_keys, expert_ids_turns).reshape((TOKENS, TOP))
    swap_plan = draw_swap_plan(jax.random.fold_in(splits[6], 71), 0)
    down_weight = scatter_about(splits[4], (EXPERTS, FF, D), FF ** -0.5, 0.1875, ((0, 64), (2, 8)))
    out_grad = scatter_about(splits[5], (TOKENS, D), 0.05, 0.29882812, ((0, 512),))
    return {"hidden": hidden, "probs": probs, "expert_ids": expert_ids, "swap_plan": swap_plan, "down_weight": down_weight, "out_grad": out_grad}


def reference(hidden, probs, expert_ids, swap_plan, down_weight, out_grad):
    experts = EXPERTS
    blocks = TOKENS // TOK_DEV
    per_block = TOK_DEV * TOP
    numbers = jnp.arange(experts, dtype=jnp.int32)
    owner = jnp.where(swap_plan == 1, (numbers + experts // 2) % experts, numbers).astype(jnp.int32)
    routed = expert_ids.reshape(blocks, per_block)
    marks = (routed[:, :, None] == numbers[None, None, :]).astype(jnp.int32)
    rank = jnp.sum((jnp.cumsum(marks, axis=1) - marks) * marks, axis=2)
    target = routed * (blocks * CAP) + jnp.arange(blocks, dtype=jnp.int32)[:, None] * CAP + rank
    target = target.reshape(-1).astype(jnp.int32)
    count = experts * blocks * CAP
    table = jnp.full((count,), -1, jnp.int32).at[target].set(jnp.arange(blocks * per_block, dtype=jnp.int32))
    filled = (table >= 0)[:, None]
    pick = jnp.maximum(table, 0).astype(jnp.int32)
    hidden_rows = hidden.reshape(blocks * per_block, FF)
    hidden_buf = (hidden_rows[pick] * filled.astype(hidden.dtype)).reshape(experts, blocks * CAP, FF)

    def forward(pair):
        rows, weight = pair
        return jnp.dot(rows, weight, preferred_element_type=jnp.float32).astype(jnp.bfloat16)

    out_buf = lax.map(forward, (hidden_buf, down_weight))
    slot_out = out_buf.reshape(count, D)[target].reshape(TOKENS, TOP, D)
    slot_wide = slot_out.astype(jnp.float32)
    mixed = jnp.sum(probs[:, :, None] * slot_wide, axis=1).astype(jnp.bfloat16)
    upstream = out_grad.astype(jnp.float32)
    prob_grad = jnp.sum(upstream[:, None, :] * slot_wide, axis=2)
    grad_rows = (probs[:, :, None] * upstream[:, None, :]).astype(jnp.bfloat16).reshape(blocks * per_block, D)
    grad_buf = (grad_rows[pick] * filled.astype(grad_rows.dtype)).reshape(experts, blocks * CAP, D)

    def backward(triple):
        rows, grads, weight = triple
        grads3 = grads.astype(jnp.float32).reshape(-1, N_DP, D // N_DP)
        weight3 = weight.astype(jnp.float32).reshape(FF, N_DP, D // N_DP)
        parts = jnp.einsum("rjc,fjc->jrf", grads3, weight3)
        parts = lax.optimization_barrier(parts.astype(jnp.bfloat16)).astype(jnp.float32)
        summed = jnp.sum(parts, axis=0).astype(jnp.bfloat16)
        expert_grad = lax.dot_general(rows, grads, (((0,), (0,)), ((), ())), preferred_element_type=jnp.float32).astype(jnp.bfloat16)
        return summed, expert_grad

    hidden_buf_grad, expert_grad = lax.map(backward, (hidden_buf, grad_buf, down_weight))
    hidden_grad = hidden_buf_grad.reshape(count, FF)[target].reshape(TOKENS, TOP, FF)
    weight_grad = expert_grad[owner]
    return mixed, hidden_grad, prob_grad, weight_grad
```

```python
import functools

import jax
import jax.numpy as jnp
from jax import lax
from jax.experimental import pallas as pl
from jax.experimental.pallas import tpu as pltpu
from jax.sharding import PartitionSpec as P

MESH = pl.DeviceIdType.MESH
RUNS = 4
CAP = 4
BF16, F32 = jnp.bfloat16, jnp.float32


def dot(a, b, dims):
    return lax.dot_general(a, b, (dims, ((), ())), preferred_element_type=F32)


def done(view, sem):
    pltpu.make_async_copy(view, view, sem).wait()


def kernel(
    sizes, hid, og, probs, codes, flag, w, mixed, hgrad, pgrad, wgrad,
    hs, gs, hz, gz, cz, hx, gx, hr, hr2, gr, place, w2, ox, ot, ou, oz,
    ps, pk, pr, px, pt, pu, pz, dsend, dkeep, drecv,
    z_send, z_recv, x_send, x_recv, b_send, b_recv, p_send, p_recv,
):
    xys, low, tok = sizes
    chips = RUNS * low
    near = 2 * low
    half = hid.shape[1] // 2
    cols = w.shape[1]
    quads = near // 2
    e, d = lax.axis_index("expert"), lax.axis_index("dp")
    zh, xy, zl, c = e // xys, e % xys, d // 2, d % 2
    z = zh * low + zl
    other = 1 - c

    def at_chip(step, core):
        to = (z + step + chips) % chips
        return (to // low) * xys + xy, (to % low) * 2 + core

    far = low * (1 - 2 * c)
    partner = ((zh + RUNS // 2) % RUNS * xys + xy, d)
    sibling = (e, zl * 2 + other)

    def in_plane(n):
        to = (xy + n) % xys
        return to, (zh * xys + to, d)

    def remote(src, dst, ssem, rsem, to):
        return pltpu.make_async_remote_copy(
            src_ref=src, dst_ref=dst, send_sem=ssem, recv_sem=rsem, device_id=to, device_id_type=MESH
        )

    barrier = pltpu.get_barrier_semaphore()

    def greet(to):
        pl.semaphore_signal(barrier, inc=1, device_id=to, device_id_type=MESH)

    def step_of(i):
        return jnp.where(i < low - 1, i - (low - 1), i - (low - 2))

    def hello_z(i, _):
        for core in range(2):
            greet(at_chip(step_of(i), core))
        return 0

    def hello_xy(n, _):
        greet(in_plane(n)[1])
        return 0

    lax.fori_loop(0, near - 2, hello_z, 0)
    for core in range(2):
        greet(at_chip(low, core))
        greet(at_chip(-low, core))
    greet(sibling)
    greet(partner)
    lax.fori_loop(1, xys, hello_xy, 0)
    pl.semaphore_wait(barrier, 2 * (near - 2) + 4 + 2 + xys - 1)

    def z_out(src_of, dst, k):
        def one(step, slot, core):
            remote(src_of(step, core), dst.at[slot * 2 + c], z_send.at[k], z_recv.at[k], at_chip(step, core)).start()

        def go(i, _):
            step = step_of(i)
            for core in range(2):
                one(step, low - 1 - step, core)
            return 0

        lax.fori_loop(0, near - 2, go, 0)
        for core in range(2):
            one(far, near - 1, core)
        mine = (low - 1) * 2 + c
        remote(src_of(0, other), dst.at[mine], z_send.at[k], z_recv.at[k], sibling).start()
        pltpu.make_async_copy(src_of(0, c), dst.at[mine], z_recv.at[k]).start()

    def z_back(src, dst, k):
        def one(step, slot, core, to):
            remote(src.at[slot * 2 + core], dst.at[(low - 1 - step) * 2 + c], z_send.at[k], z_recv.at[k], to).start()

        def go(i, _):
            step = step_of(i)
            for core in range(2):
                one(step, step + low - 1, core, at_chip(step, core))
            return 0

        lax.fori_loop(0, near - 2, go, 0)
        for core in range(2):
            remote(
                src.at[(near - 1) * 2 + core], dst.at[(near - 1) * 2 + c], z_send.at[k], z_recv.at[k],
                at_chip(low * (2 * core - 1), core),
            ).start()
        one(0, low - 1, other, sibling)
        pltpu.make_async_copy(src.at[(low - 1) * 2 + c], dst.at[(low - 1) * 2 + c], z_recv.at[k]).start()

    def x_out(src, dst, k):
        def go(n, _):
            to, dev = in_plane(n)
            remote(src.at[to], dst.at[xy], x_send.at[k], x_recv.at[k], dev).start()
            return 0

        lax.fori_loop(1, xys, go, 0)
        pltpu.make_async_copy(src.at[xy], dst.at[xy], x_recv.at[k]).start()

    z_out(lambda step, core: codes, cz, 0)
    for h in range(2):
        hs[h] = hid[:, h * half : (h + 1) * half]
    z_out(lambda step, core: hs.at[core], hz, 1)
    for g in range(gs.shape[0]):
        up = og[:, g * cols : (g + 1) * cols].astype(F32)
        gs[g] = (probs[...] * up).astype(BF16)
    z_out(lambda step, core: gs.at[((zl + step + low) % low) * 2 + core], gz, 2)

    done(cz, z_recv.at[0])
    rows = xys * 32
    row = lax.broadcasted_iota(jnp.int32, (rows, tok), 0)
    side = (row // 16) % 2
    holder = (zh + side * (RUNS // 2)) % RUNS
    wanted = ((holder * xys + row // 32) * CAP + row % CAP).astype(F32)
    source = (row // CAP) % 4

    def build(q, _):
        for m in range(4):
            code = cz[4 * q + m][0:1, :].astype(F32)
            hit = jnp.where((wanted == code) & (source == m), 1.0, 0.0)
            place[q, :, m * tok : (m + 1) * tok] = hit.astype(BF16)
        return 0

    lax.fori_loop(0, quads, build, 0)

    def put(src, dst):
        def one(q, _):
            block = src[pl.ds(4 * q, 4)].reshape(4 * tok, src.shape[2])
            out = dot(place[q], block, ((1,), (0,))).astype(BF16)
            dst[:, :, pl.ds(pl.multiple_of(q * 16, 16), 16), :] = out.reshape(xys, 2, 16, src.shape[2])
            return 0

        lax.fori_loop(0, quads, one, 0)

    def take(src, dst):
        def one(q, _):
            block = src[:, :, pl.ds(pl.multiple_of(q * 16, 16), 16), :].reshape(rows, src.shape[3])
            out = dot(place[q], block, ((0,), (0,))).astype(BF16)
            dst[pl.ds(4 * q, 4)] = out.reshape(4, tok, src.shape[3])
            return 0

        lax.fori_loop(0, quads, one, 0)

    done(hz, z_recv.at[1])
    put(hz, hx)
    x_out(hx, hr, 0)
    done(gz, z_recv.at[2])
    weights = remote(w, w2, p_send.at[0], p_recv.at[0], partner)
    weights.start()
    put(gz, gx)
    x_out(gx, gr, 1)

    done(hr, x_recv.at[0])
    halves = remote(hr, hr2, b_send.at[0], b_recv.at[0], sibling)
    halves.start()
    done(gr, x_recv.at[1])
    halves.wait_recv()

    blocks = min(4, xys)
    per = xys // blocks
    slots = near * 2 * CAP
    mine_at = pl.multiple_of(c * half, half)
    other_at = pl.multiple_of(other * half, half)

    def chunk(ref, b, s):
        return ref[pl.ds(b * per, per), s].reshape(per * slots, ref.shape[3])

    def forward(wref, s):
        def one(b, _):
            out = dot(chunk(hr, b, s), wref[pl.ds(mine_at, half), :], ((1,), (0,)))
            out += dot(chunk(hr2, b, s), wref[pl.ds(other_at, half), :], ((1,), (0,)))
            ox[pl.ds(b * per, per), s] = out.astype(BF16).reshape(per, slots, cols)
            return 0

        lax.fori_loop(0, blocks, one, 0)

    def backward(wref, s):
        def one(b, _):
            g = chunk(gr, b, s)
            keep = dot(g, wref[pl.ds(mine_at, half), :], ((1,), (1,))).astype(BF16)
            give = dot(g, wref[pl.ds(other_at, half), :], ((1,), (1,))).astype(BF16)
            pk[pl.ds(b * per, per), s] = keep.reshape(per, slots, half)
            ps[pl.ds(b * per, per), s] = give.reshape(per, slots, half)
            return 0

        lax.fori_loop(0, blocks, one, 0)

    part = min(256, half)
    swapped = flag[0:1, 0:1] > 0.5

    def outer(ref, start):
        def one(i, _):
            at = pl.multiple_of(i * part, part)
            sums = []
            for s in range(2):
                lhs = ref[:, s, :, pl.ds(at, part)].reshape(xys * slots, part)
                sums.append(dot(lhs, gr[:, s].reshape(xys * slots, cols), ((0,), (0,))))
            to = pl.ds(pl.multiple_of(start + at, part), part)
            dsend[to, :] = jnp.where(swapped, sums[0], sums[1]).astype(BF16)
            dkeep[to, :] = jnp.where(swapped, sums[1], sums[0])
            return 0

        lax.fori_loop(0, half // part, one, 0)

    forward(w, 0)
    backward(w, 0)
    outer(hr, c * half)
    outer(hr2, other * half)
    grads = remote(dsend, drecv, p_send.at[1], p_recv.at[1], partner)
    grads.start()

    weights.wait_recv()
    backward(w2, 1)
    partial = remote(ps, pr, b_send.at[1], b_recv.at[1], sibling)
    partial.start()
    forward(w2, 1)
    x_out(ox, ot, 2)
    partial.wait_recv()

    def pair(b, _):
        at = pl.ds(b * per, per)
        px[at] = (pk[at].astype(F32) + pr[at].astype(F32)).astype(BF16)
        return 0

    lax.fori_loop(0, blocks, pair, 0)
    x_out(px, pt, 3)
    done(ot, x_recv.at[2])
    take(ot, ou)
    z_back(ou, oz, 3)
    done(pt, x_recv.at[3])
    take(pt, pu)
    z_back(pu, pz, 4)

    grads.wait_recv()
    wgrad[...] = (dkeep[...] + drecv[...].astype(F32)).astype(BF16)

    done(oz, z_recv.at[3])
    total = jnp.zeros((tok, 1), F32)
    for k in range(low):
        first = (k + low - 1) * 2
        second = (near - 1) * 2 if k == 0 else (k - 1) * 2
        for core in range(2):
            value = oz[first + core].astype(F32) + oz[second + core].astype(F32)
            at = pl.ds(pl.multiple_of((((zl + k) % low) * 2 + core) * cols, cols), cols)
            mixed[:, at] = (probs[...] * value).astype(BF16)
            total += jnp.sum(og[:, at].astype(F32) * value, axis=1, keepdims=True)
    pgrad[...] = total

    done(pz, z_recv.at[4])
    for core in range(2):
        value = pz[core].astype(F32)
        for k in range(1, near):
            value += pz[2 * k + core].astype(F32)
        hgrad[:, core * half : (core + 1) * half] = value.astype(BF16)

    for k, ref in enumerate((cz, hz, gz, oz, pz)):
        done(ref.at[pl.ds(0, 2 * near - 1)], z_send.at[k])
    for k, ref in enumerate((hr, gr, ot, pt)):
        done(ref.at[pl.ds(0, xys - 1)], x_send.at[k])
    halves.wait_send()
    partial.wait_send()
    weights.wait_send()
    grads.wait_send()


def shards(xys, low, hidden, probs, expert_ids, swap_plan, down_weight, out_grad):
    tok, _, width_ff = hidden.shape
    width = out_grad.shape[1]
    cols = down_weight.shape[2]
    half = width_ff // 2
    near = 2 * low
    slots = near * 2 * CAP
    mine = lax.axis_index("expert")
    ids = expert_ids[:, 0]
    order = jnp.arange(tok, dtype=jnp.int32)
    before = (ids[:, None] == ids[None, :]) & (order[:, None] < order[None, :])
    code = ids * CAP + jnp.sum(before.astype(jnp.int32), axis=0)
    codes = jnp.broadcast_to(code.astype(F32)[None, :], (16, tok)).astype(BF16)
    experts = swap_plan.shape[0]
    own = jnp.sum(jnp.where(jnp.arange(experts, dtype=jnp.int32) == mine, swap_plan, 0))
    flag = jnp.broadcast_to((own == 1).astype(F32), (8, 128))
    vm = pl.BlockSpec(memory_space=pltpu.VMEM)
    S = jax.ShapeDtypeStruct
    V = pltpu.VMEM
    plane_h, plane_g = (xys, 2, slots, half), (xys, 2, slots, cols)
    line_h, line_g = (2 * near, tok, half), (2 * near, tok, cols)
    dma = pltpu.SemaphoreType.DMA
    mixed, hgrad, pgrad, wgrad = pl.pallas_call(
        functools.partial(kernel, (xys, low, tok)),
        out_shape=(
            S((tok, width), BF16),
            S((tok, width_ff), BF16),
            S((tok, 1), F32),
            S((width_ff, cols), BF16),
        ),
        in_specs=[vm] * 6,
        out_specs=(vm,) * 4,
        scratch_shapes=[
            V((2, tok, half), BF16), V((2 * low, tok, cols), BF16),
            V(line_h, BF16), V(line_g, BF16), V((2 * near, 16, tok), BF16),
            V(plane_h, BF16), V(plane_g, BF16), V(plane_h, BF16), V(plane_h, BF16), V(plane_g, BF16),
            V((near // 2, xys * 32, 4 * tok), BF16), V((width_ff, cols), BF16),
            V(plane_g, BF16), V(plane_g, BF16), V(line_g, BF16), V(line_g, BF16),
            V(plane_h, BF16), V(plane_h, BF16), V(plane_h, BF16), V(plane_h, BF16), V(plane_h, BF16),
            V(line_h, BF16), V(line_h, BF16),
            V((width_ff, cols), BF16), V((width_ff, cols), F32), V((width_ff, cols), BF16),
            dma((5,)), dma((5,)), dma((4,)), dma((4,)), dma((2,)), dma((2,)), dma((2,)), dma((2,)),
        ],
        compiler_params=pltpu.CompilerParams(
            collective_id=0, has_side_effects=True, vmem_limit_bytes=60 << 20
        ),
    )(hidden[:, 0, :], out_grad, probs, codes, flag, down_weight[0])
    return mixed, hgrad[:, None, :], pgrad, wgrad[None]


def solution(mesh):
    experts, groups = mesh.shape["expert"], mesh.shape["dp"]
    tokens, line = P(("expert", "dp"), None), P(("expert", "dp"), None, None)
    weights = P("expert", None, "dp")
    return jax.shard_map(
        functools.partial(shards, experts // RUNS, groups // 2),
        mesh=mesh,
        in_specs=(line, tokens, tokens, P(), weights, tokens),
        out_specs=(tokens, line, tokens, weights),
        check_vma=False,
    )
```

```python
import functools

import jax
import jax.numpy as jnp
from jax import lax
from jax.experimental import pallas as pl
from jax.experimental.pallas import tpu as pltpu
from jax.sharding import PartitionSpec as P

MESH = pl.DeviceIdType.MESH
RUNS = 4
CAP = 4
BF16, F32 = jnp.bfloat16, jnp.float32


def dot(a, b, dims):
    return lax.dot_general(a, b, (dims, ((), ())), preferred_element_type=F32)


def done(view, sem):
    pltpu.make_async_copy(view, view, sem).wait()


def kernel(
    sizes, hid, og, probs, codes, flag, w, mixed, hgrad, pgrad, wgrad,
    hs, hs2, gs, hz, gz, cz, xs, xr, hr2, place, w2, rs, rt, ou, oz,
    ps, pk, pr, pu, pz, dsend, dkeep, drecv,
    c_send, c_recv, g_send, g_recv, o_send, o_recv, x_send, x_recv, y_send, y_recv,
    b_send, b_recv, s_send, s_recv, t_send, t_recv, p_send, p_recv, h_send, h_recv, f_send, f_recv,
):
    xys, low, tok = sizes
    chips = RUNS * low
    near = 2 * low
    half = hid.shape[1] // 2
    cols = w.shape[1]
    quads = near // 2
    e, d = lax.axis_index("expert"), lax.axis_index("dp")
    zh, xy, zl, c = e // xys, e % xys, d // 2, d % 2
    z = zh * low + zl
    other = 1 - c

    def at_chip(step, core):
        to = (z + step + chips) % chips
        return (to // low) * xys + xy, (to % low) * 2 + core

    far = low * (1 - 2 * c)
    partner = ((zh + RUNS // 2) % RUNS * xys + xy, d)
    sibling = (e, zl * 2 + other)

    def in_plane(n):
        to = (xy + n) % xys
        return to, (zh * xys + to, d)

    def remote(src, dst, ssem, rsem, to):
        return pltpu.make_async_remote_copy(
            src_ref=src, dst_ref=dst, send_sem=ssem, recv_sem=rsem, device_id=to, device_id_type=MESH
        )

    barrier = pltpu.get_barrier_semaphore()

    def greet(to):
        pl.semaphore_signal(barrier, inc=1, device_id=to, device_id_type=MESH)

    def step_of(i):
        return jnp.where(i < low - 1, i - (low - 1), i - (low - 2))

    def hello_z(i, _):
        for core in range(2):
            greet(at_chip(step_of(i), core))
        return 0

    def hello_xy(n, _):
        greet(in_plane(n)[1])
        return 0

    lax.fori_loop(0, near - 2, hello_z, 0)
    for core in range(2):
        greet(at_chip(low, core))
        greet(at_chip(-low, core))
    greet(sibling)
    greet(partner)
    lax.fori_loop(1, xys, hello_xy, 0)
    pl.semaphore_wait(barrier, 2 * (near - 2) + 4 + 2 + xys - 1)

    centre = (low - 1) * 2
    rows = xys * 32
    last_step = {slot: slot - low + 1 for slot in range(near - 1)}
    level = {**{slot: abs(step) for slot, step in last_step.items()}, near - 1: low}
    order = sorted(range(quads), key=lambda q: max(level[2 * q], level[2 * q + 1]))
    mine_at = pl.multiple_of(c * half, half)
    other_at = pl.multiple_of(other * half, half)
    right, left = pl.ds(half, cols), pl.ds(0, half)

    def band(q):
        return pl.ds(q * 16, 16)

    def in_quad(q, ref):
        return ref.at[pl.ds(4 * q, 4)]

    def z_out(src_of, dst, ssem, rsem, levels):
        def one(step, slot, core):
            remote(src_of(step, core), dst.at[slot * 2 + c], ssem, rsem(slot // 2), at_chip(step, core)).start()

        for k in levels:
            if k == 0:
                pltpu.make_async_copy(src_of(0, c), dst.at[centre + c], rsem((low - 1) // 2)).start()
                remote(src_of(0, other), dst.at[centre + c], ssem, rsem((low - 1) // 2), sibling).start()
            elif k < low:
                for step in (k, -k):
                    for core in range(2):
                        one(step, low - 1 - step, core)
            else:
                for core in range(2):
                    one(far, near - 1, core)

    def z_back(q):
        def one(step, slot, core, to):
            remote(ou.at[slot * 2 + core], oz.at[(low - 1 - step) * 2 + c], o_send, o_recv, to).start()

        for slot in (2 * q, 2 * q + 1):
            if slot == near - 1:
                for core in range(2):
                    remote(
                        ou.at[slot * 2 + core], oz.at[slot * 2 + c], o_send, o_recv,
                        at_chip(low * (2 * core - 1), core),
                    ).start()
            elif slot == low - 1:
                one(0, slot, other, sibling)
                pltpu.make_async_copy(ou.at[slot * 2 + c], oz.at[slot * 2 + c], o_recv).start()
            else:
                for core in range(2):
                    one(last_step[slot], slot, core, at_chip(last_step[slot], core))

    def x_out(src, dst, q, ssem, rsem):
        def go(n, _):
            to, dev = in_plane(n)
            remote(src.at[to, :, band(q)], dst.at[xy, :, band(q)], ssem, rsem, dev).start()
            return 0

        lax.fori_loop(1, xys, go, 0)
        pltpu.make_async_copy(src.at[xy, :, band(q)], dst.at[xy, :, band(q)], rsem).start()

    hs[...] = hid[:, pl.ds(other_at, half)]
    mates = remote(hs, hz.at[centre + c], b_send.at[0], b_recv.at[0], sibling)
    mates.start()
    hz[centre + c] = hid[:, pl.ds(mine_at, half)]

    def hop(way, k):
        if k == low:
            src, dst = (hz.at[0], hz.at[2 * near - 2]) if way > 0 else (hz.at[2 * near - 3], hz.at[2 * near - 1])
        else:
            src, dst = (centre - 2 * way * (k - 1)), (centre - 2 * way * k)
            src, dst = hz.at[pl.ds(src, 2)], hz.at[pl.ds(dst, 2)]
        n = 0 if way > 0 else 1
        return remote(src, dst, h_send.at[n, k - 1], h_recv.at[n, k - 1], at_chip(way, c))

    z_out(lambda step, core: codes, cz, c_send, lambda q: c_recv, range(low + 1))
    mates.wait_recv()
    for way in (1, -1):
        hop(way, 1).start()
    for g in range(gs.shape[0]):
        up = og[:, g * cols : (g + 1) * cols].astype(F32)
        gs[g] = (probs[...] * up).astype(BF16)

    def g_out(*levels):
        z_out(
            lambda step, core: gs.at[((zl + step + low) % low) * 2 + core], gz, g_send, lambda q: g_recv.at[q], levels
        )

    g_out(0, 1)

    done(cz, c_recv)
    row = lax.broadcasted_iota(jnp.int32, (rows, tok), 0)
    side = (row // 16) % 2
    holder = (zh + side * (RUNS // 2)) % RUNS
    wanted = ((holder * xys + row // 32) * CAP + row % CAP).astype(F32)
    source = (row // CAP) % 4

    def build(q, _):
        for m in range(4):
            code = cz[4 * q + m][0:1, :].astype(F32)
            hit = jnp.where((wanted == code) & (source == m), 1.0, 0.0)
            place[q, :, m * tok : (m + 1) * tok] = hit.astype(BF16)
        return 0

    lax.fori_loop(0, quads, build, 0)

    def put(src, q, at):
        block = src[pl.ds(4 * q, 4)].reshape(4 * tok, src.shape[2])
        out = dot(place[q], block, ((1,), (0,))).astype(BF16)
        xs[:, :, band(q), at] = out.reshape(xys, 2, 16, src.shape[2])

    def take(q, at, dst):
        block = rt[:, :, band(q), at].reshape(rows, dst.shape[2])
        out = dot(place[q], block, ((0,), (0,))).astype(BF16)
        dst[pl.ds(4 * q, 4)] = out.reshape(4, tok, dst.shape[2])

    def halves(q):
        return remote(
            xr.at[:, :, band(q), left], hr2.at[:, :, band(q)], s_send.at[q], s_recv.at[q], sibling
        )

    def chunk(ref, q, s, at):
        return ref[:, s, band(q), at].reshape(xys * 16, half)

    def forward(wref, q, s):
        out = dot(chunk(xr, q, s, left), wref[pl.ds(mine_at, half), :], ((1,), (0,)))
        out += dot(chunk(hr2, q, s, left), wref[pl.ds(other_at, half), :], ((1,), (0,)))
        rs[:, s, band(q), left] = out.astype(BF16).reshape(xys, 16, cols)

    def backward(wref, q, s):
        g = chunk(xr, q, s, right)
        keep = dot(g, wref[pl.ds(mine_at, half), :], ((1,), (1,))).astype(BF16)
        give = dot(g, wref[pl.ds(other_at, half), :], ((1,), (1,))).astype(BF16)
        pk[:, s, band(q)] = keep.reshape(xys, 16, half)
        ps[:, s, band(q)] = give.reshape(xys, 16, half)

    def arrive(q):
        done(xr.at[:, :, band(q)], x_recv.at[q])
        halves(q).start()

    def own(q):
        backward(w, q, 0)
        halves(q).wait_recv()
        forward(w, q, 0)

    weights = remote(w, w2, p_send.at[0], p_recv.at[0], partner)
    for n, q in enumerate(order):
        for way in (1, -1):
            hop(way, n + 1).wait_recv()
        if n + 1 < low:
            for way in (1, -1):
                hop(way, n + 2).start()
            g_out(n + 2)
        if n == max(low - 2, 0):
            weights.start()
        put(hz, q, left)
        done(in_quad(q, gz), g_recv.at[q])
        put(gz, q, right)
        x_out(xs, xr, q, x_send.at[q], x_recv.at[q])
        if n > 0:
            arrive(order[n - 1])
        if n > 1:
            own(order[n - 2])
    arrive(order[-1])
    for q in order[-2:]:
        own(q)

    slots = near * 2 * CAP
    part = min(256, half)
    swapped = flag[0:1, 0:1] > 0.5

    def outer(ref, start):
        def one(i, _):
            at = pl.multiple_of(i * part, part)
            sums = []
            for s in range(2):
                lhs = ref[:, s, :, pl.ds(at, part)].reshape(xys * slots, part)
                sums.append(dot(lhs, xr[:, s, :, right].reshape(xys * slots, cols), ((0,), (0,))))
            to = pl.ds(pl.multiple_of(start + at, part), part)
            dsend[to, :] = jnp.where(swapped, sums[0], sums[1]).astype(BF16)
            dkeep[to, :] = jnp.where(swapped, sums[1], sums[0])
            return 0

        lax.fori_loop(0, half // part, one, 0)

    outer(xr, c * half)
    outer(hr2, other * half)
    grads = remote(dsend, drecv, p_send.at[1], p_recv.at[1], partner)

    def partial(q):
        return remote(ps.at[:, :, band(q)], pr.at[:, :, band(q)], t_send.at[q], t_recv.at[q], sibling)

    def pair(q):
        partial(q).wait_recv()
        value = pk[:, :, band(q)].astype(F32) + pr[:, :, band(q)].astype(F32)
        rs[:, :, band(q), right] = value.astype(BF16)
        x_out(rs, rt, q, y_send.at[q], y_recv.at[q])

    weights.wait_recv()
    grads.start()
    back = order[::-1]
    for n, q in enumerate(back):
        backward(w2, q, 1)
        partial(q).start()
        forward(w2, q, 1)
        if n > 0:
            pair(back[n - 1])
    pair(back[-1])

    def fold(way, k):
        n = 0 if way > 0 else 1
        if k == low:
            src = pu.at[pl.ds(2 * near - 1, 1)] if way > 0 else pu.at[pl.ds(2 * near - 2, 1)]
            dst = pz.at[n, 0, pl.ds(0, 1)]
        else:
            src, dst = pu.at[pl.ds(centre + 2 * way * k, 2)], pz.at[n, low - k]
        return remote(src, dst, f_send.at[n, k - 1], f_recv.at[n, k - 1], at_chip(way, c))

    def add(way, k):
        n = 0 if way > 0 else 1
        fold(way, k + 1).wait_recv()
        if k + 1 == low:
            at = centre + 2 * way * k + 1 - n
            pu[at] = (pu[at].astype(F32) + pz[n, 0, 0].astype(F32)).astype(BF16)
        else:
            at = pl.ds(centre + 2 * way * k, 2)
            pu[at] = (pu[at].astype(F32) + pz[n, low - k - 1].astype(F32)).astype(BF16)

    for n, q in enumerate(back):
        done(rt.at[:, :, band(q)], y_recv.at[q])
        take(q, right, pu)
        for way in (1, -1):
            if n > 0:
                add(way, low - n)
            fold(way, low - n).start()
        take(q, left, ou)
        z_back(q)
    for way in (1, -1):
        add(way, 0)
    last = remote(pu.at[centre + other], hs2, b_send.at[1], b_recv.at[1], sibling)
    last.start()
    hgrad[:, pl.ds(mine_at, half)] = pu[centre + c]

    grads.wait_recv()
    wgrad[...] = (dkeep[...] + drecv[...].astype(F32)).astype(BF16)

    done(oz, o_recv)
    total = jnp.zeros((tok, 1), F32)
    for k in range(low):
        first = (k + low - 1) * 2
        second = (near - 1) * 2 if k == 0 else (k - 1) * 2
        for core in range(2):
            value = oz[first + core].astype(F32) + oz[second + core].astype(F32)
            at = pl.ds(pl.multiple_of((((zl + k) % low) * 2 + core) * cols, cols), cols)
            mixed[:, at] = (probs[...] * value).astype(BF16)
            total += jnp.sum(og[:, at].astype(F32) * value, axis=1, keepdims=True)
    pgrad[...] = total
    last.wait_recv()
    hgrad[:, pl.ds(other_at, half)] = hs2[...]

    for ref, sem in ((cz, c_send), (gz, g_send), (oz, o_send)):
        done(ref.at[pl.ds(0, 2 * near - 1)], sem)
    for way in (1, -1):
        for k in range(1, low + 1):
            hop(way, k).wait_send()
            fold(way, k).wait_send()
    for q in range(quads):
        done(xr.at[pl.ds(0, xys - 1), :, band(q)], x_send.at[q])
        done(rt.at[pl.ds(0, xys - 1), :, band(q)], y_send.at[q])
        halves(q).wait_send()
        partial(q).wait_send()
    mates.wait_send()
    last.wait_send()
    weights.wait_send()
    grads.wait_send()


def shards(xys, low, hidden, probs, expert_ids, swap_plan, down_weight, out_grad):
    tok, _, width_ff = hidden.shape
    width = out_grad.shape[1]
    cols = down_weight.shape[2]
    half = width_ff // 2
    near = 2 * low
    slots = near * 2 * CAP
    mine = lax.axis_index("expert")
    ids = expert_ids[:, 0]
    order = jnp.arange(tok, dtype=jnp.int32)
    before = (ids[:, None] == ids[None, :]) & (order[:, None] < order[None, :])
    code = ids * CAP + jnp.sum(before.astype(jnp.int32), axis=0)
    codes = jnp.broadcast_to(code.astype(F32)[None, :], (16, tok)).astype(BF16)
    experts = swap_plan.shape[0]
    own = jnp.sum(jnp.where(jnp.arange(experts, dtype=jnp.int32) == mine, swap_plan, 0))
    flag = jnp.broadcast_to((own == 1).astype(F32), (8, 128))
    vm = pl.BlockSpec(memory_space=pltpu.VMEM)
    S = jax.ShapeDtypeStruct
    V = pltpu.VMEM
    plane, wide = (xys, 2, slots, half), (xys, 2, slots, half + cols)
    line_h, line_g = (2 * near, tok, half), (2 * near, tok, cols)
    dma = pltpu.SemaphoreType.DMA
    quads = near // 2
    mixed, hgrad, pgrad, wgrad = pl.pallas_call(
        functools.partial(kernel, (xys, low, tok)),
        out_shape=(
            S((tok, width), BF16),
            S((tok, width_ff), BF16),
            S((tok, 1), F32),
            S((width_ff, cols), BF16),
        ),
        in_specs=[vm] * 6,
        out_specs=(vm,) * 4,
        scratch_shapes=[
            V((tok, half), BF16), V((tok, half), BF16), V((2 * low, tok, cols), BF16),
            V(line_h, BF16), V(line_g, BF16), V((2 * near, 16, tok), BF16),
            V(wide, BF16), V(wide, BF16), V(plane, BF16),
            V((quads, xys * 32, 4 * tok), BF16), V((width_ff, cols), BF16),
            V(wide, BF16), V(wide, BF16), V(line_g, BF16), V(line_g, BF16),
            V(plane, BF16), V(plane, BF16), V(plane, BF16),
            V(line_h, BF16), V((2, low, 2, tok, half), BF16),
            V((width_ff, cols), BF16), V((width_ff, cols), F32), V((width_ff, cols), BF16),
            dma, dma, dma, dma((quads,)), dma, dma,
            dma((quads,)), dma((quads,)), dma((quads,)), dma((quads,)), dma((2,)), dma((2,)),
            dma((quads,)), dma((quads,)), dma((quads,)), dma((quads,)), dma((2,)), dma((2,)),
            dma((2, low)), dma((2, low)), dma((2, low)), dma((2, low)),
        ],
        compiler_params=pltpu.CompilerParams(
            collective_id=0, has_side_effects=True, vmem_limit_bytes=60 << 20
        ),
    )(hidden[:, 0, :], out_grad, probs, codes, flag, down_weight[0])
    return mixed, hgrad[:, None, :], pgrad, wgrad[None]


def solution(mesh):
    experts, groups = mesh.shape["expert"], mesh.shape["dp"]
    tokens, line = P(("expert", "dp"), None), P(("expert", "dp"), None, None)
    weights = P("expert", None, "dp")
    return jax.shard_map(
        functools.partial(shards, experts // RUNS, groups // 2),
        mesh=mesh,
        in_specs=(line, tokens, tokens, P(), weights, tokens),
        out_specs=(tokens, line, tokens, weights),
        check_vma=False,
    )
```

```python
import functools

import jax
import jax.numpy as jnp
from jax import lax
from jax.experimental import pallas as pl
from jax.experimental.pallas import tpu as pltpu
from jax.sharding import PartitionSpec as P

MESH = pl.DeviceIdType.MESH
RUNS = 4
CAP = 4
BF16, F32 = jnp.bfloat16, jnp.float32


def dot(a, b, dims):
    return lax.dot_general(a, b, (dims, ((), ())), preferred_element_type=F32)


def done(view, sem):
    pltpu.make_async_copy(view, view, sem).wait()


def kernel(
    sizes, hid, og, weight_row, ids, plan, w, mixed, hgrad, pgrad, wgrad,
    codes, probs,
    hs, hs2, gs, hz, gz, cz, xs, xr, hr2, place, w2, rs, rt, ou, oz,
    ps, pk, pr, pu, pz, dsend, dkeep, drecv,
    c_send, c_recv, g_send, g_recv, o_send, o_recv, x_send, x_recv, y_send, y_recv,
    b_send, b_recv, s_send, s_recv, t_send, t_recv, p_send, p_recv, h_send, h_recv, f_send, f_recv,
):
    xys, low, tok = sizes
    chips = RUNS * low
    near = 2 * low
    half = hid.shape[1] // 2
    cols = w.shape[1]
    quads = near // 2
    e, d = lax.axis_index("expert"), lax.axis_index("dp")
    zh, xy, zl, c = e // xys, e % xys, d // 2, d % 2
    z = zh * low + zl
    other = 1 - c

    def at_chip(step, core):
        to = (z + step + chips) % chips
        return (to // low) * xys + xy, (to % low) * 2 + core

    far = low * (1 - 2 * c)
    partner = ((zh + RUNS // 2) % RUNS * xys + xy, d)
    sibling = (e, zl * 2 + other)

    def in_plane(n):
        to = (xy + n) % xys
        return to, (zh * xys + to, d)

    def remote(src, dst, ssem, rsem, to):
        return pltpu.make_async_remote_copy(
            src_ref=src, dst_ref=dst, send_sem=ssem, recv_sem=rsem, device_id=to, device_id_type=MESH
        )

    barrier = pltpu.get_barrier_semaphore()

    def greet(to):
        pl.semaphore_signal(barrier, inc=1, device_id=to, device_id_type=MESH)

    def step_of(i):
        return jnp.where(i < low - 1, i - (low - 1), i - (low - 2))

    def hello_z(i, _):
        for core in range(2):
            greet(at_chip(step_of(i), core))
        return 0

    def hello_xy(n, _):
        greet(in_plane(n)[1])
        return 0

    lax.fori_loop(0, near - 2, hello_z, 0)
    for core in range(2):
        greet(at_chip(low, core))
        greet(at_chip(-low, core))
    greet(sibling)
    greet(partner)
    lax.fori_loop(1, xys, hello_xy, 0)

    centre = (low - 1) * 2
    rows = xys * 32
    last_step = {slot: slot - low + 1 for slot in range(near - 1)}
    level = {**{slot: abs(step) for slot, step in last_step.items()}, near - 1: low}
    order = sorted(range(quads), key=lambda q: max(level[2 * q], level[2 * q + 1]))
    mine_at = pl.multiple_of(c * half, half)
    other_at = pl.multiple_of(other * half, half)
    right, left = pl.ds(half, cols), pl.ds(0, half)

    def band(q):
        return pl.ds(q * 16, 16)

    def in_quad(q, ref):
        return ref.at[pl.ds(4 * q, 4)]

    def z_out(src_of, dst, ssem, rsem, levels):
        def one(step, slot, core):
            remote(src_of(step, core), dst.at[slot * 2 + c], ssem, rsem(slot // 2), at_chip(step, core)).start()

        for k in levels:
            if k == 0:
                pltpu.make_async_copy(src_of(0, c), dst.at[centre + c], rsem((low - 1) // 2)).start()
                remote(src_of(0, other), dst.at[centre + c], ssem, rsem((low - 1) // 2), sibling).start()
            elif k < low:
                for step in (k, -k):
                    for core in range(2):
                        one(step, low - 1 - step, core)
            else:
                for core in range(2):
                    one(far, near - 1, core)

    def z_back(q):
        def one(step, slot, core, to):
            remote(ou.at[slot * 2 + core], oz.at[(low - 1 - step) * 2 + c], o_send, o_recv, to).start()

        for slot in (2 * q, 2 * q + 1):
            if slot == near - 1:
                for core in range(2):
                    remote(
                        ou.at[slot * 2 + core], oz.at[slot * 2 + c], o_send, o_recv,
                        at_chip(low * (2 * core - 1), core),
                    ).start()
            elif slot == low - 1:
                one(0, slot, other, sibling)
                pltpu.make_async_copy(ou.at[slot * 2 + c], oz.at[slot * 2 + c], o_recv).start()
            else:
                for core in range(2):
                    one(last_step[slot], slot, core, at_chip(last_step[slot], core))

    def x_out(src, dst, q, ssem, rsem):
        def go(n, _):
            to, dev = in_plane(n)
            remote(src.at[to, :, band(q)], dst.at[xy, :, band(q)], ssem, rsem, dev).start()
            return 0

        lax.fori_loop(1, xys, go, 0)
        pltpu.make_async_copy(src.at[xy, :, band(q)], dst.at[xy, :, band(q)], rsem).start()

    hs[...] = hid[:, pl.ds(other_at, half)]
    hz[centre + c] = hid[:, pl.ds(mine_at, half)]
    named = jnp.broadcast_to(ids[...].astype(F32), (tok, tok))
    earlier = lax.broadcasted_iota(jnp.int32, (tok, tok), 0) < lax.broadcasted_iota(jnp.int32, (tok, tok), 1)
    rank = jnp.sum(jnp.where((named == named.T) & earlier, 1.0, 0.0), axis=0, keepdims=True)
    codes[...] = jnp.broadcast_to(ids[...].astype(F32) * CAP + rank, codes.shape).astype(BF16)
    probs[...] = jnp.broadcast_to(weight_row[...], (tok, tok)).T[:, 0:1]
    pl.semaphore_wait(barrier, 2 * (near - 2) + 4 + 2 + xys - 1)
    mates = remote(hs, hz.at[centre + c], b_send.at[0], b_recv.at[0], sibling)
    mates.start()

    def hop(way, k):
        if k == low:
            src, dst = (hz.at[0], hz.at[2 * near - 2]) if way > 0 else (hz.at[2 * near - 3], hz.at[2 * near - 1])
        else:
            src, dst = (centre - 2 * way * (k - 1)), (centre - 2 * way * k)
            src, dst = hz.at[pl.ds(src, 2)], hz.at[pl.ds(dst, 2)]
        n = 0 if way > 0 else 1
        return remote(src, dst, h_send.at[n, k - 1], h_recv.at[n, k - 1], at_chip(way, c))

    z_out(lambda step, core: codes, cz, c_send, lambda q: c_recv, range(low + 1))
    mates.wait_recv()
    for way in (1, -1):
        hop(way, 1).start()
    for g in range(gs.shape[0]):
        up = og[:, g * cols : (g + 1) * cols].astype(F32)
        gs[g] = (probs[...] * up).astype(BF16)

    def g_out(*levels):
        z_out(
            lambda step, core: gs.at[((zl + step + low) % low) * 2 + core], gz, g_send, lambda q: g_recv.at[q], levels
        )

    g_out(0, 1)

    done(cz, c_recv)
    row = lax.broadcasted_iota(jnp.int32, (rows, tok), 0)
    side = (row // 16) % 2
    holder = (zh + side * (RUNS // 2)) % RUNS
    wanted = ((holder * xys + row // 32) * CAP + row % CAP).astype(F32)
    source = (row // CAP) % 4

    def build(q, _):
        for m in range(4):
            code = cz[4 * q + m][0:1, :].astype(F32)
            hit = jnp.where((wanted == code) & (source == m), 1.0, 0.0)
            place[q, :, m * tok : (m + 1) * tok] = hit.astype(BF16)
        return 0

    lax.fori_loop(0, quads, build, 0)

    def put(src, q, at):
        block = src[pl.ds(4 * q, 4)].reshape(4 * tok, src.shape[2])
        out = dot(place[q], block, ((1,), (0,))).astype(BF16)
        xs[:, :, band(q), at] = out.reshape(xys, 2, 16, src.shape[2])

    def take(q, at, dst):
        block = rt[:, :, band(q), at].reshape(rows, dst.shape[2])
        out = dot(place[q], block, ((0,), (0,))).astype(BF16)
        dst[pl.ds(4 * q, 4)] = out.reshape(4, tok, dst.shape[2])

    def halves(q):
        return remote(
            xr.at[:, :, band(q), left], hr2.at[:, :, band(q)], s_send.at[q], s_recv.at[q], sibling
        )

    def chunk(ref, q, s, at):
        return ref[:, s, band(q), at].reshape(xys * 16, half)

    def forward(wref, q, s):
        out = dot(chunk(xr, q, s, left), wref[pl.ds(mine_at, half), :], ((1,), (0,)))
        out += dot(chunk(hr2, q, s, left), wref[pl.ds(other_at, half), :], ((1,), (0,)))
        rs[:, s, band(q), left] = out.astype(BF16).reshape(xys, 16, cols)

    def backward(wref, q, s):
        g = chunk(xr, q, s, right)
        keep = dot(g, wref[pl.ds(mine_at, half), :], ((1,), (1,))).astype(BF16)
        give = dot(g, wref[pl.ds(other_at, half), :], ((1,), (1,))).astype(BF16)
        pk[:, s, band(q)] = keep.reshape(xys, 16, half)
        ps[:, s, band(q)] = give.reshape(xys, 16, half)

    def arrive(q):
        done(xr.at[:, :, band(q)], x_recv.at[q])
        halves(q).start()

    def own(q):
        backward(w, q, 0)
        halves(q).wait_recv()
        forward(w, q, 0)

    weights = remote(w, w2, p_send.at[0], p_recv.at[0], partner)
    for n, q in enumerate(order):
        for way in (1, -1):
            hop(way, n + 1).wait_recv()
        if n + 1 < low:
            for way in (1, -1):
                hop(way, n + 2).start()
            g_out(n + 2)
        if n == max(low - 2, 0):
            weights.start()
        put(hz, q, left)
        done(in_quad(q, gz), g_recv.at[q])
        put(gz, q, right)
        x_out(xs, xr, q, x_send.at[q], x_recv.at[q])
        if n > 0:
            arrive(order[n - 1])
        if n > 1:
            own(order[n - 2])
    arrive(order[-1])
    for q in order[-2:]:
        own(q)

    slots = near * 2 * CAP
    part = min(256, half)
    held = lax.broadcasted_iota(jnp.int32, plan.shape, 1) == e
    swapped = jnp.sum(jnp.where(held, plan[...].astype(F32), 0.0), axis=1, keepdims=True) == 1.0

    def outer(ref, start):
        def one(i, _):
            at = pl.multiple_of(i * part, part)
            sums = []
            for s in range(2):
                lhs = ref[:, s, :, pl.ds(at, part)].reshape(xys * slots, part)
                sums.append(dot(lhs, xr[:, s, :, right].reshape(xys * slots, cols), ((0,), (0,))))
            to = pl.ds(pl.multiple_of(start + at, part), part)
            dsend[to, :] = jnp.where(swapped, sums[0], sums[1]).astype(BF16)
            dkeep[to, :] = jnp.where(swapped, sums[1], sums[0])
            return 0

        lax.fori_loop(0, half // part, one, 0)

    outer(xr, c * half)
    outer(hr2, other * half)
    grads = remote(dsend, drecv, p_send.at[1], p_recv.at[1], partner)

    def partial(q):
        return remote(ps.at[:, :, band(q)], pr.at[:, :, band(q)], t_send.at[q], t_recv.at[q], sibling)

    def pair(q):
        partial(q).wait_recv()
        value = pk[:, :, band(q)].astype(F32) + pr[:, :, band(q)].astype(F32)
        rs[:, :, band(q), right] = value.astype(BF16)
        x_out(rs, rt, q, y_send.at[q], y_recv.at[q])

    weights.wait_recv()
    grads.start()
    back = order[::-1]
    for n, q in enumerate(back):
        backward(w2, q, 1)
        partial(q).start()
        forward(w2, q, 1)
        if n > 0:
            pair(back[n - 1])
    pair(back[-1])

    def fold(way, k):
        n = 0 if way > 0 else 1
        if k == low:
            src = pu.at[pl.ds(2 * near - 1, 1)] if way > 0 else pu.at[pl.ds(2 * near - 2, 1)]
            dst = pz.at[n, 0, pl.ds(0, 1)]
        else:
            src, dst = pu.at[pl.ds(centre + 2 * way * k, 2)], pz.at[n, low - k]
        return remote(src, dst, f_send.at[n, k - 1], f_recv.at[n, k - 1], at_chip(way, c))

    def add(way, k):
        n = 0 if way > 0 else 1
        fold(way, k + 1).wait_recv()
        if k + 1 == low:
            at = centre + 2 * way * k + 1 - n
            pu[at] = (pu[at].astype(F32) + pz[n, 0, 0].astype(F32)).astype(BF16)
        else:
            at = pl.ds(centre + 2 * way * k, 2)
            pu[at] = (pu[at].astype(F32) + pz[n, low - k - 1].astype(F32)).astype(BF16)

    for n, q in enumerate(back):
        done(rt.at[:, :, band(q)], y_recv.at[q])
        take(q, right, pu)
        for way in (1, -1):
            if n > 0:
                add(way, low - n)
            fold(way, low - n).start()
        take(q, left, ou)
        z_back(q)
    for way in (1, -1):
        add(way, 0)
    last = remote(pu.at[centre + other], hs2, b_send.at[1], b_recv.at[1], sibling)
    last.start()
    hgrad[:, pl.ds(mine_at, half)] = pu[centre + c]

    grads.wait_recv()
    wgrad[...] = (dkeep[...] + drecv[...].astype(F32)).astype(BF16)

    done(oz, o_recv)
    total = jnp.zeros((tok, 1), F32)
    for k in range(low):
        first = (k + low - 1) * 2
        second = (near - 1) * 2 if k == 0 else (k - 1) * 2
        for core in range(2):
            value = oz[first + core].astype(F32) + oz[second + core].astype(F32)
            at = pl.ds(pl.multiple_of((((zl + k) % low) * 2 + core) * cols, cols), cols)
            mixed[:, at] = (probs[...] * value).astype(BF16)
            total += jnp.sum(og[:, at].astype(F32) * value, axis=1, keepdims=True)
    pgrad[...] = jnp.broadcast_to(total, (tok, tok)).T[0:1, :]
    last.wait_recv()
    hgrad[:, pl.ds(other_at, half)] = hs2[...]

    for ref, sem in ((cz, c_send), (gz, g_send), (oz, o_send)):
        done(ref.at[pl.ds(0, 2 * near - 1)], sem)
    for way in (1, -1):
        for k in range(1, low + 1):
            hop(way, k).wait_send()
            fold(way, k).wait_send()
    for q in range(quads):
        done(xr.at[pl.ds(0, xys - 1), :, band(q)], x_send.at[q])
        done(rt.at[pl.ds(0, xys - 1), :, band(q)], y_send.at[q])
        halves(q).wait_send()
        partial(q).wait_send()
    mates.wait_send()
    last.wait_send()
    weights.wait_send()
    grads.wait_send()


def shards(xys, low, hidden, probs, expert_ids, swap_plan, down_weight, out_grad):
    tok, _, width_ff = hidden.shape
    width = out_grad.shape[1]
    cols = down_weight.shape[2]
    half = width_ff // 2
    near = 2 * low
    slots = near * 2 * CAP
    vm = pl.BlockSpec(memory_space=pltpu.VMEM)
    S = jax.ShapeDtypeStruct
    V = pltpu.VMEM
    plane, wide = (xys, 2, slots, half), (xys, 2, slots, half + cols)
    line_h, line_g = (2 * near, tok, half), (2 * near, tok, cols)
    dma = pltpu.SemaphoreType.DMA
    quads = near // 2
    mixed, hgrad, pgrad, wgrad = pl.pallas_call(
        functools.partial(kernel, (xys, low, tok)),
        out_shape=(
            S((tok, width), BF16),
            S((tok, width_ff), BF16),
            S((1, tok), F32),
            S((width_ff, cols), BF16),
        ),
        in_specs=[vm] * 6,
        out_specs=(vm,) * 4,
        scratch_shapes=[
            V((16, tok), BF16), V((tok, 1), F32),
            V((tok, half), BF16), V((tok, half), BF16), V((2 * low, tok, cols), BF16),
            V(line_h, BF16), V(line_g, BF16), V((2 * near, 16, tok), BF16),
            V(wide, BF16), V(wide, BF16), V(plane, BF16),
            V((quads, xys * 32, 4 * tok), BF16), V((width_ff, cols), BF16),
            V(wide, BF16), V(wide, BF16), V(line_g, BF16), V(line_g, BF16),
            V(plane, BF16), V(plane, BF16), V(plane, BF16),
            V(line_h, BF16), V((2, low, 2, tok, half), BF16),
            V((width_ff, cols), BF16), V((width_ff, cols), F32), V((width_ff, cols), BF16),
            dma, dma, dma, dma((quads,)), dma, dma,
            dma((quads,)), dma((quads,)), dma((quads,)), dma((quads,)), dma((2,)), dma((2,)),
            dma((quads,)), dma((quads,)), dma((quads,)), dma((quads,)), dma((2,)), dma((2,)),
            dma((2, low)), dma((2, low)), dma((2, low)), dma((2, low)),
        ],
        compiler_params=pltpu.CompilerParams(
            collective_id=0, has_side_effects=True, vmem_limit_bytes=60 << 20
        ),
    )(hidden[:, 0, :], out_grad, probs.reshape(1, tok), expert_ids.reshape(1, tok), swap_plan.reshape(1, -1), down_weight[0])
    return mixed, hgrad[:, None, :], pgrad.reshape(tok, 1), wgrad[None]


def solution(mesh):
    experts, groups = mesh.shape["expert"], mesh.shape["dp"]
    tokens, line = P(("expert", "dp"), None), P(("expert", "dp"), None, None)
    weights = P("expert", None, "dp")
    return jax.shard_map(
        functools.partial(shards, experts // RUNS, groups // 2),
        mesh=mesh,
        in_specs=(line, tokens, tokens, P(), weights, tokens),
        out_specs=(tokens, line, tokens, weights),
        check_vma=False,
    )
```

```python
import functools

import jax
import jax.numpy as jnp
from jax import lax
from jax.experimental import pallas as pl
from jax.experimental.pallas import tpu as pltpu
from jax.sharding import PartitionSpec as P

MESH = pl.DeviceIdType.MESH
RUNS = 4
CAP = 4
BF16, F32 = jnp.bfloat16, jnp.float32


def dot(a, b, dims):
    return lax.dot_general(a, b, (dims, ((), ())), preferred_element_type=F32)


def done(view, sem):
    pltpu.make_async_copy(view, view, sem).wait()


def kernel(
    sizes, hid, og, weight_row, ids, plan, w, mixed, hgrad, pgrad, wgrad,
    codes, probs,
    hs, hs2, gs, hz, gz, cz, xs, xr, hr2, place, w2, rs, rt, ou, oz,
    ps, pk, pr, pu, pz, dsend, dkeep, drecv,
    c_send, c_recv, g_send, g_recv, o_send, o_recv, x_send, x_recv, y_send, y_recv,
    b_send, b_recv, s_send, s_recv, t_send, t_recv, p_send, p_recv, h_send, h_recv, f_send, f_recv,
):
    xys, low, tok = sizes
    chips = RUNS * low
    near = 2 * low
    half = hid.shape[1] // 2
    cols = w.shape[1]
    quads = near // 2
    e, d = lax.axis_index("expert"), lax.axis_index("dp")
    zh, xy, zl, c = e // xys, e % xys, d // 2, d % 2
    z = zh * low + zl
    other = 1 - c

    def at_chip(step, core):
        to = (z + step + chips) % chips
        return (to // low) * xys + xy, (to % low) * 2 + core

    far = low * (1 - 2 * c)
    partner = ((zh + RUNS // 2) % RUNS * xys + xy, d)
    sibling = (e, zl * 2 + other)

    def in_plane(n):
        to = (xy + n) % xys
        return to, (zh * xys + to, d)

    def remote(src, dst, ssem, rsem, to):
        return pltpu.make_async_remote_copy(
            src_ref=src, dst_ref=dst, send_sem=ssem, recv_sem=rsem, device_id=to, device_id_type=MESH
        )

    barrier = pltpu.get_barrier_semaphore()

    def greet(to):
        pl.semaphore_signal(barrier, inc=1, device_id=to, device_id_type=MESH)

    def step_of(i):
        return jnp.where(i < low - 1, i - (low - 1), i - (low - 2))

    def hello_z(i, _):
        for core in range(2):
            greet(at_chip(step_of(i), core))
        return 0

    def hello_xy(n, _):
        greet(in_plane(n)[1])
        return 0

    lax.fori_loop(0, near - 2, hello_z, 0)
    for core in range(2):
        greet(at_chip(low, core))
        greet(at_chip(-low, core))
    greet(sibling)
    greet(partner)
    lax.fori_loop(1, xys, hello_xy, 0)

    centre = (low - 1) * 2
    rows = xys * 32
    last_step = {slot: slot - low + 1 for slot in range(near - 1)}
    level = {**{slot: abs(step) for slot, step in last_step.items()}, near - 1: low}
    order = sorted(range(quads), key=lambda q: max(level[2 * q], level[2 * q + 1]))
    mine_at = pl.multiple_of(c * half, half)
    other_at = pl.multiple_of(other * half, half)
    right, left = pl.ds(half, cols), pl.ds(0, half)

    def band(q):
        return pl.ds(q * 16, 16)

    def in_quad(q, ref):
        return ref.at[pl.ds(4 * q, 4)]

    def z_out(src_of, dst, ssem, rsem, levels):
        def one(step, slot, core):
            remote(src_of(step, core), dst.at[slot * 2 + c], ssem, rsem(slot // 2), at_chip(step, core)).start()

        for k in levels:
            if k == 0:
                pltpu.make_async_copy(src_of(0, c), dst.at[centre + c], rsem((low - 1) // 2)).start()
                remote(src_of(0, other), dst.at[centre + c], ssem, rsem((low - 1) // 2), sibling).start()
            elif k < low:
                for step in (k, -k):
                    for core in range(2):
                        one(step, low - 1 - step, core)
            else:
                for core in range(2):
                    one(far, near - 1, core)

    def z_back(q):
        def one(step, slot, core, to):
            remote(ou.at[slot * 2 + core], oz.at[(low - 1 - step) * 2 + c], o_send, o_recv, to).start()

        for slot in (2 * q, 2 * q + 1):
            if slot == near - 1:
                for core in range(2):
                    remote(
                        ou.at[slot * 2 + core], oz.at[slot * 2 + c], o_send, o_recv,
                        at_chip(low * (2 * core - 1), core),
                    ).start()
            elif slot == low - 1:
                one(0, slot, other, sibling)
                pltpu.make_async_copy(ou.at[slot * 2 + c], oz.at[slot * 2 + c], o_recv).start()
            else:
                for core in range(2):
                    one(last_step[slot], slot, core, at_chip(last_step[slot], core))

    def x_out(src, dst, q, ssem, rsem):
        def go(n, _):
            to, dev = in_plane(n)
            remote(src.at[to, :, band(q)], dst.at[xy, :, band(q)], ssem, rsem, dev).start()
            return 0

        lax.fori_loop(1, xys, go, 0)
        pltpu.make_async_copy(src.at[xy, :, band(q)], dst.at[xy, :, band(q)], rsem).start()

    hs[...] = hid[:, pl.ds(other_at, half)]
    hz[centre + c] = hid[:, pl.ds(mine_at, half)]
    named = jnp.broadcast_to(ids[...].astype(F32), (tok, tok))
    earlier = lax.broadcasted_iota(jnp.int32, (tok, tok), 0) < lax.broadcasted_iota(jnp.int32, (tok, tok), 1)
    rank = jnp.sum(jnp.where((named == named.T) & earlier, 1.0, 0.0), axis=0, keepdims=True)
    codes[...] = jnp.broadcast_to(ids[...].astype(F32) * CAP + rank, codes.shape).astype(BF16)
    probs[...] = jnp.broadcast_to(weight_row[...], (tok, tok)).T[:, 0:1]
    pl.semaphore_wait(barrier, 2 * (near - 2) + 4 + 2 + xys - 1)
    mates = remote(hs, hz.at[centre + c], b_send.at[0], b_recv.at[0], sibling)
    mates.start()

    def hop(way, k, part):
        lines = pl.ds(part * (tok // 2), tok // 2)
        if k == low:
            src, dst = (0, 2 * near - 2) if way > 0 else (2 * near - 3, 2 * near - 1)
            src, dst = hz.at[src, lines], hz.at[dst, lines]
        else:
            src, dst = (centre - 2 * way * (k - 1)), (centre - 2 * way * k)
            src, dst = hz.at[pl.ds(src, 2), lines], hz.at[pl.ds(dst, 2), lines]
        n = 0 if way > 0 else 1
        return remote(src, dst, h_send.at[n, k - 1, part], h_recv.at[n, k - 1, part], at_chip(way, c))

    z_out(lambda step, core: codes, cz, c_send, lambda q: c_recv, range(low + 1))
    mates.wait_recv()
    for part in range(2):
        for way in (1, -1):
            hop(way, 1, part).start()
    for g in range(gs.shape[0]):
        up = og[:, g * cols : (g + 1) * cols].astype(F32)
        gs[g] = (probs[...] * up).astype(BF16)

    def g_out(*levels):
        z_out(
            lambda step, core: gs.at[((zl + step + low) % low) * 2 + core], gz, g_send, lambda q: g_recv.at[q], levels
        )

    g_out(0, 1)

    done(cz, c_recv)
    row = lax.broadcasted_iota(jnp.int32, (rows, tok), 0)
    side = (row // 16) % 2
    holder = (zh + side * (RUNS // 2)) % RUNS
    wanted = ((holder * xys + row // 32) * CAP + row % CAP).astype(F32)
    source = (row // CAP) % 4

    def build(q, _):
        for m in range(4):
            code = cz[4 * q + m][0:1, :].astype(F32)
            hit = jnp.where((wanted == code) & (source == m), 1.0, 0.0)
            place[q, :, m * tok : (m + 1) * tok] = hit.astype(BF16)
        return 0

    lax.fori_loop(0, quads, build, 0)

    def put(src, q, at):
        block = src[pl.ds(4 * q, 4)].reshape(4 * tok, src.shape[2])
        out = dot(place[q], block, ((1,), (0,))).astype(BF16)
        xs[:, :, band(q), at] = out.reshape(xys, 2, 16, src.shape[2])

    def take(q, at, dst):
        block = rt[:, :, band(q), at].reshape(rows, dst.shape[2])
        out = dot(place[q], block, ((0,), (0,))).astype(BF16)
        dst[pl.ds(4 * q, 4)] = out.reshape(4, tok, dst.shape[2])

    def halves(q):
        return remote(
            xr.at[:, :, band(q), left], hr2.at[:, :, band(q)], s_send.at[q], s_recv.at[q], sibling
        )

    def chunk(ref, q, s, at):
        return ref[:, s, band(q), at].reshape(xys * 16, half)

    def forward(wref, q, s):
        out = dot(chunk(xr, q, s, left), wref[pl.ds(mine_at, half), :], ((1,), (0,)))
        out += dot(chunk(hr2, q, s, left), wref[pl.ds(other_at, half), :], ((1,), (0,)))
        rs[:, s, band(q), left] = out.astype(BF16).reshape(xys, 16, cols)

    def backward(wref, q, s):
        g = chunk(xr, q, s, right)
        keep = dot(g, wref[pl.ds(mine_at, half), :], ((1,), (1,))).astype(BF16)
        give = dot(g, wref[pl.ds(other_at, half), :], ((1,), (1,))).astype(BF16)
        pk[:, s, band(q)] = keep.reshape(xys, 16, half)
        ps[:, s, band(q)] = give.reshape(xys, 16, half)

    def arrive(q):
        done(xr.at[:, :, band(q)], x_recv.at[q])
        halves(q).start()

    def own(q):
        backward(w, q, 0)
        halves(q).wait_recv()
        forward(w, q, 0)

    weights = remote(w, w2, p_send.at[0], p_recv.at[0], partner)
    for n, q in enumerate(order):
        for part in range(2):
            for way in (1, -1):
                hop(way, n + 1, part).wait_recv()
                if n + 1 < low:
                    hop(way, n + 2, part).start()
        if n + 1 < low:
            g_out(n + 2)
        if n == max(low - 2, 0):
            weights.start()
        put(hz, q, left)
        done(in_quad(q, gz), g_recv.at[q])
        put(gz, q, right)
        x_out(xs, xr, q, x_send.at[q], x_recv.at[q])
        if n > 0:
            arrive(order[n - 1])
        if n > 1:
            own(order[n - 2])
    arrive(order[-1])
    for q in order[-2:]:
        own(q)

    slots = near * 2 * CAP
    part = min(256, half)
    held = lax.broadcasted_iota(jnp.int32, plan.shape, 1) == e
    swapped = jnp.sum(jnp.where(held, plan[...].astype(F32), 0.0), axis=1, keepdims=True) == 1.0

    def outer(ref, start):
        def one(i, _):
            at = pl.multiple_of(i * part, part)
            sums = []
            for s in range(2):
                lhs = ref[:, s, :, pl.ds(at, part)].reshape(xys * slots, part)
                sums.append(dot(lhs, xr[:, s, :, right].reshape(xys * slots, cols), ((0,), (0,))))
            to = pl.ds(pl.multiple_of(start + at, part), part)
            dsend[to, :] = jnp.where(swapped, sums[0], sums[1]).astype(BF16)
            dkeep[to, :] = jnp.where(swapped, sums[1], sums[0])
            return 0

        lax.fori_loop(0, half // part, one, 0)

    outer(xr, c * half)
    outer(hr2, other * half)
    grads = remote(dsend, drecv, p_send.at[1], p_recv.at[1], partner)

    def partial(q):
        return remote(ps.at[:, :, band(q)], pr.at[:, :, band(q)], t_send.at[q], t_recv.at[q], sibling)

    def pair(q):
        partial(q).wait_recv()
        value = pk[:, :, band(q)].astype(F32) + pr[:, :, band(q)].astype(F32)
        rs[:, :, band(q), right] = value.astype(BF16)
        x_out(rs, rt, q, y_send.at[q], y_recv.at[q])

    weights.wait_recv()
    grads.start()
    back = order[::-1]
    for n, q in enumerate(back):
        backward(w2, q, 1)
        partial(q).start()
        forward(w2, q, 1)
        if n > 0:
            pair(back[n - 1])
    pair(back[-1])

    def fold(way, k):
        n = 0 if way > 0 else 1
        if k == low:
            src = pu.at[pl.ds(2 * near - 1, 1)] if way > 0 else pu.at[pl.ds(2 * near - 2, 1)]
            dst = pz.at[n, 0, pl.ds(0, 1)]
        else:
            src, dst = pu.at[pl.ds(centre + 2 * way * k, 2)], pz.at[n, low - k]
        return remote(src, dst, f_send.at[n, k - 1], f_recv.at[n, k - 1], at_chip(way, c))

    def add(way, k):
        n = 0 if way > 0 else 1
        fold(way, k + 1).wait_recv()
        if k + 1 == low:
            at = centre + 2 * way * k + 1 - n
            pu[at] = (pu[at].astype(F32) + pz[n, 0, 0].astype(F32)).astype(BF16)
        else:
            at = pl.ds(centre + 2 * way * k, 2)
            pu[at] = (pu[at].astype(F32) + pz[n, low - k - 1].astype(F32)).astype(BF16)

    for n, q in enumerate(back):
        done(rt.at[:, :, band(q)], y_recv.at[q])
        take(q, right, pu)
        for way in (1, -1):
            if n > 0:
                add(way, low - n)
            fold(way, low - n).start()
        take(q, left, ou)
        z_back(q)
    for way in (1, -1):
        add(way, 0)
    last = remote(pu.at[centre + other], hs2, b_send.at[1], b_recv.at[1], sibling)
    last.start()
    hgrad[:, pl.ds(mine_at, half)] = pu[centre + c]

    grads.wait_recv()
    wgrad[...] = (dkeep[...] + drecv[...].astype(F32)).astype(BF16)

    done(oz, o_recv)
    total = jnp.zeros((tok, 1), F32)
    for k in range(low):
        first = (k + low - 1) * 2
        second = (near - 1) * 2 if k == 0 else (k - 1) * 2
        for core in range(2):
            value = oz[first + core].astype(F32) + oz[second + core].astype(F32)
            at = pl.ds(pl.multiple_of((((zl + k) % low) * 2 + core) * cols, cols), cols)
            mixed[:, at] = (probs[...] * value).astype(BF16)
            total += jnp.sum(og[:, at].astype(F32) * value, axis=1, keepdims=True)
    pgrad[...] = jnp.broadcast_to(total, (tok, tok)).T[0:1, :]
    last.wait_recv()
    hgrad[:, pl.ds(other_at, half)] = hs2[...]

    for ref, sem in ((cz, c_send), (gz, g_send), (oz, o_send)):
        done(ref.at[pl.ds(0, 2 * near - 1)], sem)
    for way in (1, -1):
        for k in range(1, low + 1):
            for part in range(2):
                hop(way, k, part).wait_send()
            fold(way, k).wait_send()
    for q in range(quads):
        done(xr.at[pl.ds(0, xys - 1), :, band(q)], x_send.at[q])
        done(rt.at[pl.ds(0, xys - 1), :, band(q)], y_send.at[q])
        halves(q).wait_send()
        partial(q).wait_send()
    mates.wait_send()
    last.wait_send()
    weights.wait_send()
    grads.wait_send()


def shards(xys, low, hidden, probs, expert_ids, swap_plan, down_weight, out_grad):
    tok, _, width_ff = hidden.shape
    width = out_grad.shape[1]
    cols = down_weight.shape[2]
    half = width_ff // 2
    near = 2 * low
    slots = near * 2 * CAP
    vm = pl.BlockSpec(memory_space=pltpu.VMEM)
    S = jax.ShapeDtypeStruct
    V = pltpu.VMEM
    plane, wide = (xys, 2, slots, half), (xys, 2, slots, half + cols)
    line_h, line_g = (2 * near, tok, half), (2 * near, tok, cols)
    dma = pltpu.SemaphoreType.DMA
    quads = near // 2
    mixed, hgrad, pgrad, wgrad = pl.pallas_call(
        functools.partial(kernel, (xys, low, tok)),
        out_shape=(
            S((tok, width), BF16),
            S((tok, width_ff), BF16),
            S((1, tok), F32),
            S((width_ff, cols), BF16),
        ),
        in_specs=[vm] * 6,
        out_specs=(vm,) * 4,
        scratch_shapes=[
            V((16, tok), BF16), V((tok, 1), F32),
            V((tok, half), BF16), V((tok, half), BF16), V((2 * low, tok, cols), BF16),
            V(line_h, BF16), V(line_g, BF16), V((2 * near, 16, tok), BF16),
            V(wide, BF16), V(wide, BF16), V(plane, BF16),
            V((quads, xys * 32, 4 * tok), BF16), V((width_ff, cols), BF16),
            V(wide, BF16), V(wide, BF16), V(line_g, BF16), V(line_g, BF16),
            V(plane, BF16), V(plane, BF16), V(plane, BF16),
            V(line_h, BF16), V((2, low, 2, tok, half), BF16),
            V((width_ff, cols), BF16), V((width_ff, cols), F32), V((width_ff, cols), BF16),
            dma, dma, dma, dma((quads,)), dma, dma,
            dma((quads,)), dma((quads,)), dma((quads,)), dma((quads,)), dma((2,)), dma((2,)),
            dma((quads,)), dma((quads,)), dma((quads,)), dma((quads,)), dma((2,)), dma((2,)),
            dma((2, low, 2)), dma((2, low, 2)), dma((2, low)), dma((2, low)),
        ],
        compiler_params=pltpu.CompilerParams(
            collective_id=0, has_side_effects=True, vmem_limit_bytes=60 << 20
        ),
    )(hidden[:, 0, :], out_grad, probs.reshape(1, tok), expert_ids.reshape(1, tok), swap_plan.reshape(1, -1), down_weight[0])
    return mixed, hgrad[:, None, :], pgrad.reshape(tok, 1), wgrad[None]


def solution(mesh):
    experts, groups = mesh.shape["expert"], mesh.shape["dp"]
    tokens, line = P(("expert", "dp"), None), P(("expert", "dp"), None, None)
    weights = P("expert", None, "dp")
    return jax.shard_map(
        functools.partial(shards, experts // RUNS, groups // 2),
        mesh=mesh,
        in_specs=(line, tokens, tokens, P(), weights, tokens),
        out_specs=(tokens, line, tokens, weights),
        check_vma=False,
    )
```
